512 devices in a mesh: expert: 128 (over y, z, x_hi), hidden: 4 (over x_lo, core).
Axes of the slice: x: 4 (x_hi: 2, x_lo: 2; x = x_hi * 2 + x_lo), y: 8, z: 8, core: 2. Of those that a mesh axis runs over, the one named last changes fastest.
Arguments:
- tokens: bfloat16 [256, 256, 1280], P('expert', 'hidden'), may hold values from -400 to 400
- slot_embed: bfloat16 [128, 1280], replicated, may hold values from -1 to 1
- w_in: bfloat16 [128, 1280, 2560], P('expert', None, 'hidden'), may hold values from -0.15625 to 0.15625
- w_out: bfloat16 [128, 2560, 1280], P('expert', 'hidden'), may hold values from -0.125 to 0.125
- grad_out: bfloat16 [256, 256, 1280], P('expert', 'hidden'), may hold values from -96 to 96
Outputs:
- grad_tokens: bfloat16 [256, 256, 1280], P('expert', 'hidden')
- grad_embed: float32 [128, 1280], P('expert', 'hidden')
The draws below stay inside these ranges and needn't reach their ends.
All inputs are finite; a program needn't handle non-finite values.
Results may differ from the reference program's by a relative error of at most 0.034.
Values may be sent and summed in bfloat16 or wider, within the bound.
A program may use at most 64 MiB of HBM per device.

```python
import jax
import jax.numpy as jnp
from jax import lax

D = 1280
FF = 2560
M = 256
EXPERTS = 128
IMAGES = 256
N_HIDDEN = 4


def embed_table(key):
    table = jax.random.truncated_normal(key, -3.0, 3.0, (EXPERTS, D), jnp.float32) * D ** (-0.5)
    return table.astype(jnp.bfloat16).astype(jnp.float32)


def draw_slot_embed(key, part):
    return embed_table(key).astype(jnp.bfloat16)


def draw_tokens(key, part):
    key = jax.random.fold_in(key, 7)
    keys = jax.random.split(key, 1)
    base = jnp.clip(jax.random.normal(keys[0], (IMAGES, M, D), jnp.float32), -6.0, 6.0)
    return base.astype(jnp.bfloat16)


def steps_of(stream_key, extent, cuts, smallest, top_value):
    factor_of, own = 1.0, jax.random.fold_in(stream_key, 6)
    for position, parts in cuts:
        draws = jnp.exp(jax.random.uniform(jax.random.fold_in(own, position), (parts,), jnp.float32, smallest / len(cuts), top_value / len(cuts)))
        factor_of = factor_of * jnp.repeat(draws, extent[position] // parts).reshape([-1 if axis == position else 1 for axis in range(len(extent))])
    return factor_of


def centred(key, shape, deviation, bound, shards=(), held_as=jnp.bfloat16):
    values = jax.random.normal(key, shape, jnp.float32) * deviation
    if len(shards) > 0:
        values = steps_of(key, shape, shards, -0.22, 0.18) * values
    return jnp.clip(values, min=-bound, max=bound).astype(held_as)


def setup_inputs(seed: int = 0) -> dict:
    arg_keys = jax.random.split(jax.random.key(seed), 6)
    tokens = draw_tokens(jax.random.fold_in(arg_keys[5], 71), 0)
    slot_embed = draw_slot_embed(jax.random.fold_in(arg_keys[5], 71), 0)
    w_in = centred(arg_keys[2], (EXPERTS, D, FF), D ** -0.5, 0.15625, ((0, 128), (2, 4)))
    w_out = centred(arg_keys[3], (EXPERTS, FF, D), FF ** -0.5, 0.125, ((0, 128), (1, 4)))
    grad_out = centred(arg_keys[4], (IMAGES, M, D), 16.0, 96.0, ((0, 128), (1, 4)))
    return {"tokens": tokens, "slot_embed": slot_embed, "w_in": w_in, "w_out": w_out, "grad_out": grad_out}


half_root = 0.7071067811865476
density_scale = 0.3989422804014327


def gelu_slope(pre):
    return 0.5 * (1.0 + lax.erf(pre * half_root)) + pre * jnp.exp(-0.5 * pre * pre) * density_scale


def rounded_back(value):
    return lax.optimization_barrier(value.astype(jnp.bfloat16)).astype(jnp.float32)


def blockwise_tokens(weights, values):
    quarter = M // N_HIDDEN
    total = jnp.zeros((weights.shape[0], weights.shape[2], values.shape[2]), jnp.float32)
    for block in range(N_HIDDEN):
        low = block * quarter
        part = jnp.einsum("bms,bmd->bsd", weights[:, low:low + quarter].astype(jnp.float32),
                          values[:, low:low + quarter].astype(jnp.float32))
        total = total + rounded_back(part)
    return total.astype(jnp.bfloat16)


def expert_pass(operands):
    first_all, second_all, rows, grads = operands
    width = FF // N_HIDDEN
    out_total = jnp.zeros((rows.shape[0], rows.shape[1]), jnp.float32)
    in_total = jnp.zeros((rows.shape[0], rows.shape[1]), jnp.float32)
    for block in range(N_HIDDEN):
        low = block * width
        first = first_all[:, low:low + width]
        second = second_all[low:low + width]
        pre = jnp.dot(rows, first, preferred_element_type=jnp.float32)
        act = jax.nn.gelu(pre, approximate=False).astype(jnp.bfloat16)
        out_part = jnp.dot(act, second, preferred_element_type=jnp.float32)
        grad_act = jnp.dot(grads, second.T, preferred_element_type=jnp.float32)
        grad_pre = (grad_act * gelu_slope(pre)).astype(jnp.bfloat16)
        in_part = jnp.dot(grad_pre, first.T, preferred_element_type=jnp.float32)
        out_total = out_total + rounded_back(out_part)
        in_total = in_total + rounded_back(in_part)
    return out_total.astype(jnp.bfloat16), in_total.astype(jnp.bfloat16)


def reference(tokens, slot_embed, w_in, w_out, grad_out):
    tokens_wide = tokens.astype(jnp.float32)
    embed_wide = slot_embed.astype(jnp.float32)
    logits = jnp.einsum("bmd,sd->bms", tokens_wide, embed_wide)
    column_exp = jnp.exp(logits - jnp.max(logits, axis=1, keepdims=True))
    dispatch = column_exp / jnp.sum(column_exp, axis=1, keepdims=True)
    row_exp = jnp.exp(logits - jnp.max(logits, axis=2, keepdims=True))
    combine = row_exp / jnp.sum(row_exp, axis=2, keepdims=True)
    dispatch_low = dispatch.astype(jnp.bfloat16)
    combine_low = combine.astype(jnp.bfloat16)
    slot_rows = blockwise_tokens(dispatch_low, tokens)
    grad_rows = blockwise_tokens(combine_low, grad_out)
    slot_out, slot_grad = lax.map(expert_pass, (w_in, w_out, jnp.transpose(slot_rows, (1, 0, 2)),
                                                jnp.transpose(grad_rows, (1, 0, 2))))
    slot_out = jnp.transpose(slot_out, (1, 0, 2)).astype(jnp.float32)
    slot_grad = jnp.transpose(slot_grad, (1, 0, 2)).astype(jnp.float32)
    grad_comb = jnp.einsum("bmd,bsd->bms", grad_out.astype(jnp.float32), slot_out)
    grad_disp = jnp.einsum("bmd,bsd->bms", tokens_wide, slot_grad)
    comb_inner = jnp.sum(combine * grad_comb, axis=2, keepdims=True)
    disp_inner = jnp.sum(dispatch * grad_disp, axis=1, keepdims=True)
    grad_logit = (combine * (grad_comb - comb_inner) + dispatch * (grad_disp - disp_inner)).astype(jnp.bfloat16)
    logit_wide = grad_logit.astype(jnp.float32)
    grad_tokens = (jnp.einsum("bms,bsd->bmd", dispatch_low.astype(jnp.float32), slot_grad)
                   + jnp.einsum("bms,sd->bmd", logit_wide, embed_wide)).astype(jnp.bfloat16)
    grad_embed = jnp.einsum("bms,bmd->sd", logit_wide, tokens_wide)
    return grad_tokens, grad_embed
```

```python
import functools

import jax
import jax.numpy as jnp
from jax import lax
from jax.experimental import pallas as pl
from jax.experimental.pallas import tpu as pltpu
from jax.sharding import PartitionSpec as P

half_root = 0.7071067811865476
density_scale = 0.3989422804014327
MESH = pl.DeviceIdType.MESH
f32 = jnp.float32
bf16 = jnp.bfloat16
NT = (((1,), (1,)), ((), ()))
TN = (((0,), (0,)), ((), ()))
NN = (((1,), (0,)), ((), ()))


def mm(a, b, dims=NN):
    return lax.dot_general(a, b, dims, preferred_element_type=f32)


def gelu_parts(pre):
    cdf = 0.5 * (1.0 + lax.erf(pre * half_root))
    return pre * cdf, cdf + pre * jnp.exp(-0.5 * pre * pre) * density_scale


def kernel(
    n, stride, tok_hbm, emb_hbm, win_hbm, wout_hbm, go_hbm, gt_out, ge_out,
    tok_v, emb_v, win_v, wout_v, lg_own, lg, tok_d, go_d, tok_o,
    disp_v, comb_v, send_f, rows_f, d_own, d_core, d_chip, d_diag,
    po_send, po_recv, acc, xs_send, xs_recv, send_b, rows_b,
    gl_send, gl_recv, gt_send, ef, send_e, recv_e, fin, lsem, ssem, rsem, wsem,
):
    g = lax.axis_index("expert")
    h = lax.axis_index("hidden")
    j = h // 2
    k = h % 2
    half = tok_d.shape[2]
    tk = tok_d.shape[1]
    others = [(j, 1 - k), (1 - j, k), (1 - j, 1 - k)]

    def device(where):
        return (g, 2 * where[0] + where[1])

    def cols(core):
        return pl.ds(pl.multiple_of(core * half, 128), half)

    def remote(src, dst, s, r, where):
        return pltpu.make_async_remote_copy(
            src_ref=src, dst_ref=dst, send_sem=ssem.at[s], recv_sem=rsem.at[r],
            device_id=device(where), device_id_type=MESH,
        )

    def partner(s):
        t = lax.rem(g + lax.rem(s * stride, n), n)
        odd = lax.rem(s, 2)
        return t, 2 * (j + odd - 2 * j * odd) + k

    loads = [
        pltpu.make_async_copy(tok_hbm, tok_v, lsem.at[0]),
        pltpu.make_async_copy(emb_hbm, emb_v, lsem.at[1]),
        pltpu.make_async_copy(win_hbm.at[0], win_v, lsem.at[2]),
        pltpu.make_async_copy(wout_hbm.at[0], wout_v, lsem.at[3]),
        pltpu.make_async_copy(tok_hbm.at[j, :, cols(k)], tok_d.at[h], lsem.at[4]),
        pltpu.make_async_copy(go_hbm.at[j, :, cols(k)], go_d.at[h], lsem.at[5]),
    ]
    for load in loads:
        load.start()

    barrier = pltpu.get_barrier_semaphore()
    for where in others:
        pl.semaphore_signal(barrier, inc=1, device_id=device(where), device_id_type=MESH)

    def greet(s, carry):
        pl.semaphore_signal(barrier, inc=1, device_id=partner(s), device_id_type=MESH)
        return carry

    lax.fori_loop(1, n, greet, 0)

    loads[0].wait()
    loads[1].wait()
    for image in range(2):
        lg_own[image] = mm(tok_v[image], emb_v[...], NT)
    lg[h] = lg_own[j]
    pl.semaphore_wait(barrier, n + 2)

    tok_c, lg_c, go_c = [], [], []
    for i in (1, 2, 0):
        where = others[i]
        copy = remote(lg_own.at[where[0]], lg.at[h], i, i, where)
        copy.start()
        lg_c.append(copy)
    for i in (1, 2, 0):
        where = others[i]
        copy = remote(tok_hbm.at[where[0], :, cols(where[1])], tok_d.at[h], 3 + i, 3 + i, where)
        copy.start()
        tok_c.append(copy)
    for i in (1, 2, 0):
        where = others[i]
        copy = remote(go_hbm.at[where[0], :, cols(where[1])], go_d.at[h], 6 + i, 6 + i, where)
        copy.start()
        go_c.append(copy)

    for copy in lg_c:
        copy.wait_recv()
    logits = lg[...].reshape(4 * tk, n)
    col = jnp.exp(logits - jnp.max(logits, axis=0, keepdims=True))
    disp = col / jnp.sum(col, axis=0, keepdims=True)
    row = jnp.exp(logits - jnp.max(logits, axis=1, keepdims=True))
    comb = row / jnp.sum(row, axis=1, keepdims=True)
    disp_v[...] = disp
    comb_v[...] = comb

    for copy in tok_c:
        copy.wait_recv()
    loads[4].wait()
    tok_x = remote(tok_d, tok_o, 9, 9, others[0])
    tok_x.start()
    slot_rows = mm(disp.astype(bf16), tok_d[...].reshape(4 * tk, half), TN).astype(bf16)
    for copy in go_c:
        copy.wait_recv()
    loads[5].wait()
    grad_rows = mm(comb.astype(bf16), go_d[...].reshape(4 * tk, half), TN).astype(bf16)
    send_f[...] = jnp.stack([slot_rows, grad_rows], axis=1)

    def spread(src, dst, sem):
        own = pltpu.make_async_copy(src.at[g], dst.at[g], lsem.at[6 + sem])
        own.start()

        def step(s, carry):
            t, at = partner(s)
            pltpu.make_async_remote_copy(
                src_ref=src.at[t], dst_ref=dst.at[g], send_sem=wsem.at[2 * sem],
                recv_sem=wsem.at[2 * sem + 1], device_id=(t, at), device_id_type=MESH,
            ).start()
            return carry

        lax.fori_loop(1, n, step, 0)
        return own

    def wait_all(ref, count, sem):
        part = ref.at[pl.ds(0, count)]
        pltpu.make_async_copy(part, part, sem).wait()

    own_f = spread(send_f, rows_f, 0)
    own_f.wait()
    wait_all(rows_f, n - 1, wsem.at[1])
    loads[2].wait()
    loads[3].wait()

    d_own[0] = rows_f[:, 0, :]
    d_own[1] = rows_f[:, 1, :]
    to_chip = remote(d_own, d_chip, 10, 10, others[1])
    to_chip.start()
    to_core = remote(d_own, d_core, 11, 11, others[0])
    to_core.start()

    def expert(mine, other, index):
        mine_at = pl.ds(pl.multiple_of(k * half, 128), half)
        other_at = pl.ds(pl.multiple_of((1 - k) * half, 128), half)
        pre = mm(mine[0], win_v[mine_at, :]) + mm(other[0], win_v[other_at, :])
        ga = mm(mine[1], wout_v[:, mine_at], NT) + mm(other[1], wout_v[:, other_at], NT)
        act, slope = gelu_parts(pre)
        act = act.astype(bf16)
        gp = (ga * slope).astype(bf16)
        po_send[index, 0] = mm(act, wout_v[:, other_at]).astype(bf16)
        po_send[index, 1] = mm(gp, win_v[other_at, :], NT).astype(bf16)
        give = remote(po_send.at[index], po_recv.at[index], 13 + index, 13 + index, others[0])
        give.start()
        acc[index, 0] = mm(act, wout_v[:, mine_at])
        acc[index, 1] = mm(gp, win_v[mine_at, :], NT)
        return give

    to_core.wait_recv()
    give0 = expert(d_own, d_core, 0)
    to_chip.wait_recv()
    forward = remote(d_chip, d_diag, 12, 12, others[0])
    forward.start()
    forward.wait_recv()
    give1 = expert(d_chip, d_diag, 1)
    give1.wait_recv()
    xs_send[...] = (acc[1] + po_recv[1].astype(f32)).astype(bf16)
    cross = remote(xs_send, xs_recv, 15, 15, others[1])
    cross.start()
    give0.wait_recv()
    total = acc[0] + po_recv[0].astype(f32)
    cross.wait_recv()
    total = (total + xs_recv[...].astype(f32)).astype(bf16)
    send_b[...] = jnp.stack([total[0], total[1]], axis=1)

    own_b = spread(send_b, rows_b, 1)
    own_b.wait()
    wait_all(rows_b, n - 1, wsem.at[3])

    slot_out = rows_b[:, 0, :]
    slot_grad = rows_b[:, 1, :]
    tok2 = tok_d[...].reshape(4 * tk, half)
    go2 = go_d[...].reshape(4 * tk, half)
    disp = disp_v[...]
    comb = comb_v[...]
    gc = comb * mm(go2, slot_out, NT)
    gd = disp * mm(tok2, slot_grad, NT)
    gl = gc - comb * jnp.sum(gc, axis=1, keepdims=True)
    gl = gl + gd - disp * jnp.sum(gd, axis=0, keepdims=True)
    gl_send[...] = gl
    gl_x = remote(gl_send, gl_recv, 16, 16, others[0])
    gl_x.start()
    first = mm(disp.astype(bf16), slot_grad)
    tok_x.wait_recv()
    gl_x.wait_recv()
    gl = (gl_send[...] + gl_recv[...]).astype(bf16)

    ef[k] = mm(gl, tok2, TN)
    ef[1 - k] = mm(gl, tok_o[...].reshape(4 * tk, half), TN)
    hn = n // 2
    mine = pl.ds(pl.multiple_of(k * hn, hn), hn)
    send_e[...] = jnp.stack([ef[0, mine, :].astype(bf16), ef[1, mine, :].astype(bf16)], axis=1)
    keeper = k == g // hn
    own_e = pltpu.make_async_copy(send_e.at[lax.rem(g, hn)], recv_e.at[g], lsem.at[8])

    def send_piece(s):
        e = lax.rem(g + lax.rem(s * stride, hn), hn)
        t = k * hn + e
        odd = lax.rem(s, 2)
        pltpu.make_async_remote_copy(
            src_ref=send_e.at[e], dst_ref=recv_e.at[g], send_sem=wsem.at[4],
            recv_sem=wsem.at[5], device_id=(t, 2 * (j + odd - 2 * j * odd) + k),
            device_id_type=MESH,
        ).start()

    def piece(s, carry):
        send_piece(s)
        return carry

    lax.fori_loop(1, hn, piece, 0)

    @pl.when(keeper)
    def _():
        own_e.start()

    @pl.when(jnp.logical_not(keeper))
    def _():
        send_piece(0)

    second = mm(gl, emb_v[:, cols(k)])
    gt_send[...] = (first + second).astype(bf16).reshape(4, tk, half)
    own_t = pltpu.make_async_copy(gt_send.at[h], gt_out.at[j, :, cols(k)], lsem.at[9])
    own_t.start()
    gt_c = []
    for i in (1, 2, 0):
        where = others[i]
        copy = remote(
            gt_send.at[2 * where[0] + where[1]], gt_out.at[j, :, cols(k)], 17 + i, 17 + i, where
        )
        copy.start()
        gt_c.append(copy)

    fin_c = [remote(fin.at[j], fin.at[j], 20 + i, 23 + j, others[i]) for i in range(3)]

    @pl.when(keeper)
    def _():
        own_e.wait()
        wait_all(recv_e, n - 1, wsem.at[5])
        rows = recv_e[...].reshape(2 * n, half)
        shape = (8, 2 * n)
        pick = lax.rem(lax.broadcasted_iota(jnp.int32, shape, 1), 2)
        pick = (pick == lax.broadcasted_iota(jnp.int32, shape, 0)).astype(bf16)
        fin[j] = mm(pick, rows)[0:2, :]
        for copy in fin_c:
            copy.start()
        for copy in fin_c:
            copy.wait_send()
        wait_all(send_e, hn - 1, wsem.at[4])
        pltpu.make_async_copy(fin.at[1 - j], fin.at[1 - j], rsem.at[24 - j]).wait()

    @pl.when(jnp.logical_not(keeper))
    def _():
        wait_all(send_e, hn, wsem.at[4])
        for chip in range(2):
            pltpu.make_async_copy(fin.at[chip], fin.at[chip], rsem.at[23 + chip]).wait()

    both = fin[0] + fin[1]
    row = jnp.where(j == 0, both[0:1, :], both[1:2, :])
    quarter = half // 2
    ge_out[...] = jnp.where(k == 0, row[:, :quarter], row[:, quarter:])

    own_t.wait()
    for copy in gt_c:
        copy.wait_recv()
    for copy in lg_c + tok_c + go_c + gt_c + [
        tok_x, to_chip, to_core, give0, give1, forward, cross, gl_x
    ]:
        copy.wait_send()
    wait_all(send_f, n - 1, wsem.at[0])
    wait_all(send_b, n - 1, wsem.at[2])


def shards(n, tokens, slot_embed, w_in, w_out, grad_out):
    images, tk, width = tokens.shape
    ff = w_in.shape[2]
    half = width // 2
    hbm = pl.BlockSpec(memory_space=pl.ANY)
    vm = pltpu.VMEM
    scratch = [
        vm((images, tk, width), bf16), vm((n, width), bf16), vm((width, ff), bf16),
        vm((ff, width), bf16), vm((images, tk, n), f32), vm((4, tk, n), f32),
        vm((4, tk, half), bf16), vm((4, tk, half), bf16), vm((4, tk, half), bf16),
        vm((4 * tk, n), f32), vm((4 * tk, n), f32),
        vm((n, 2, half), bf16), vm((n, 2, half), bf16),
        vm((2, n, half), bf16), vm((2, n, half), bf16), vm((2, n, half), bf16),
        vm((2, n, half), bf16),
        vm((2, 2, n, half), bf16), vm((2, 2, n, half), bf16), vm((2, 2, n, half), f32),
        vm((2, n, half), bf16), vm((2, n, half), bf16),
        vm((n, 2, half), bf16), vm((n, 2, half), bf16),
        vm((4 * tk, n), f32), vm((4 * tk, n), f32), vm((4, tk, half), bf16),
        vm((2, n, half), f32), vm((n // 2, 2, half), bf16), vm((n, 2, half), bf16),
        vm((2, 2, half), f32),
        pltpu.SemaphoreType.DMA((10,)), pltpu.SemaphoreType.DMA((25,)),
        pltpu.SemaphoreType.DMA((25,)), pltpu.SemaphoreType.DMA((6,)),
    ]
    stride = 37 if n == 128 else 1
    return pl.pallas_call(
        functools.partial(kernel, n, stride),
        out_shape=(
            jax.ShapeDtypeStruct(tokens.shape, bf16),
            jax.ShapeDtypeStruct((1, width // 4), f32),
        ),
        in_specs=[hbm] * 5,
        out_specs=(hbm, pl.BlockSpec(memory_space=pltpu.VMEM)),
        scratch_shapes=scratch,
        compiler_params=pltpu.CompilerParams(
            collective_id=0, has_side_effects=True, vmem_limit_bytes=40 * 2**20
        ),
        cost_estimate=pl.CostEstimate(
            flops=2 * 10**9, bytes_accessed=6 * 10**6, transcendentals=10**6
        ),
    )(tokens, slot_embed, w_in, w_out, grad_out)


def solution(mesh):
    return jax.shard_map(
        functools.partial(shards, mesh.shape["expert"]),
        mesh=mesh,
        in_specs=(
            P("expert", "hidden", None),
            P(),
            P("expert", None, "hidden"),
            P("expert", "hidden", None),
            P("expert", "hidden", None),
        ),
        out_specs=(P("expert", "hidden", None), P("expert", "hidden")),
        check_vma=False,
    )
```

```python
import functools

import jax
import jax.numpy as jnp
from jax import lax
from jax.experimental import pallas as pl
from jax.experimental.pallas import tpu as pltpu
from jax.sharding import PartitionSpec as P

half_root = 0.7071067811865476
density_scale = 0.3989422804014327
MESH = pl.DeviceIdType.MESH
f32 = jnp.float32
bf16 = jnp.bfloat16
NT = (((1,), (1,)), ((), ()))
TN = (((0,), (0,)), ((), ()))
NN = (((1,), (0,)), ((), ()))


def mm(a, b, dims=NN):
    return lax.dot_general(a, b, dims, preferred_element_type=f32)


def gelu_parts(pre):
    cdf = 0.5 * (1.0 + lax.erf(pre * half_root))
    return pre * cdf, cdf + pre * jnp.exp(-0.5 * pre * pre) * density_scale


def kernel(
    n, nz, stride, tok_hbm, emb_hbm, win_hbm, wout_hbm, go_hbm, gt_out, ge_out,
    tok_v, emb_v, win_v, wout_v, lg_own, lg, tok_d, go_d, tok_o,
    disp_v, comb_v, send_f, rows_f, d_own, d_core, d_chip, d_diag,
    po_send, po_recv, acc, xs_send, xs_recv, send_b, rows_b,
    gl_send, gl_recv, gt_send, ef, send_e, recv_e, fin, lsem, ssem, rsem, wsem, here,
):
    g = lax.axis_index("expert")
    h = lax.axis_index("hidden")
    j = h // 2
    k = h % 2
    half = tok_d.shape[2]
    tk = tok_d.shape[1]
    others = [(j, 1 - k), (1 - j, k), (1 - j, 1 - k)]

    def device(where):
        return (g, 2 * where[0] + where[1])

    def cols(core):
        return pl.ds(pl.multiple_of(core * half, 128), half)

    def remote(src, dst, s, r, where):
        return pltpu.make_async_remote_copy(
            src_ref=src, dst_ref=dst, send_sem=ssem.at[s], recv_sem=rsem.at[r],
            device_id=device(where), device_id_type=MESH,
        )

    def partner(s):
        t = lax.rem(g + lax.rem(s * stride, n), n)
        odd = lax.rem(s, 2)
        return t, 2 * (j + odd - 2 * j * odd) + k

    loads = [
        pltpu.make_async_copy(tok_hbm, tok_v, lsem.at[0]),
        pltpu.make_async_copy(emb_hbm, emb_v, lsem.at[1]),
        pltpu.make_async_copy(win_hbm.at[0], win_v, lsem.at[2]),
        pltpu.make_async_copy(wout_hbm.at[0], wout_v, lsem.at[3]),
        pltpu.make_async_copy(tok_hbm.at[j, :, cols(k)], tok_d.at[h], lsem.at[4]),
        pltpu.make_async_copy(go_hbm.at[j, :, cols(k)], go_d.at[h], lsem.at[5]),
    ]
    for load in loads:
        load.start()

    zy = n // 2
    ny = zy // nz
    a = g % 2
    z = (g // 2) % nz
    y = g // (2 * nz)
    along_z = [((y * nz + (z + i) % nz) * 2 + a, h) for i in range(1, nz)]
    along_y = [((((y + i) % ny) * nz + z) * 2 + a, h) for i in range(1, ny)]
    along_x = (g + 1 - 2 * a, 2 * (1 - j) + k)

    def tell(semaphore, peer):
        pl.semaphore_signal(semaphore, inc=1, device_id=peer, device_id_type=MESH)

    barrier = pltpu.get_barrier_semaphore()
    direct = [device(where) for where in others] + along_y + along_z + [along_x]
    for peer in direct:
        tell(barrier, peer)

    loads[0].wait()
    loads[1].wait()
    for image in range(2):
        lg_own[image] = mm(tok_v[image], emb_v[...], NT)
    lg[h] = lg_own[j]
    pl.semaphore_wait(barrier, len(direct))
    for peer in along_z:
        tell(here.at[0], peer)

    tok_c, lg_c, go_c = [], [], []
    for i in (1, 2, 0):
        where = others[i]
        copy = remote(lg_own.at[where[0]], lg.at[h], i, i, where)
        copy.start()
        lg_c.append(copy)
    for i in (1, 2, 0):
        where = others[i]
        copy = remote(tok_hbm.at[where[0], :, cols(where[1])], tok_d.at[h], 3 + i, 3 + i, where)
        copy.start()
        tok_c.append(copy)
    for i in (1, 2, 0):
        where = others[i]
        copy = remote(go_hbm.at[where[0], :, cols(where[1])], go_d.at[h], 6 + i, 6 + i, where)
        copy.start()
        go_c.append(copy)

    for copy in lg_c:
        copy.wait_recv()
    logits = lg[...].reshape(4 * tk, n)
    col = jnp.exp(logits - jnp.max(logits, axis=0, keepdims=True))
    disp = col / jnp.sum(col, axis=0, keepdims=True)
    row = jnp.exp(logits - jnp.max(logits, axis=1, keepdims=True))
    comb = row / jnp.sum(row, axis=1, keepdims=True)
    disp_v[...] = disp
    comb_v[...] = comb

    for copy in tok_c:
        copy.wait_recv()
    loads[4].wait()
    tok_x = remote(tok_d, tok_o, 9, 9, others[0])
    tok_x.start()
    slot_rows = mm(disp.astype(bf16), tok_d[...].reshape(4 * tk, half), TN).astype(bf16)
    for copy in go_c:
        copy.wait_recv()
    loads[5].wait()
    grad_rows = mm(comb.astype(bf16), go_d[...].reshape(4 * tk, half), TN).astype(bf16)
    send_f[...] = jnp.stack([slot_rows, grad_rows], axis=1)

    if nz > 1:
        pl.semaphore_wait(here.at[0], nz - 1)
    tell(here.at[1], along_x)
    pl.semaphore_wait(here.at[1], 1)

    def spread(src, dst, sem):
        own = pltpu.make_async_copy(src.at[g], dst.at[g], lsem.at[6 + sem])
        own.start()

        def step(s, carry):
            t, at = partner(s)
            pltpu.make_async_remote_copy(
                src_ref=src.at[t], dst_ref=dst.at[g], send_sem=wsem.at[2 * sem],
                recv_sem=wsem.at[2 * sem + 1], device_id=(t, at), device_id_type=MESH,
            ).start()
            return carry

        lax.fori_loop(1, n, step, 0)
        return own

    def wait_all(ref, count, sem):
        part = ref.at[pl.ds(0, count)]
        pltpu.make_async_copy(part, part, sem).wait()

    own_f = spread(send_f, rows_f, 0)
    own_f.wait()
    wait_all(rows_f, n - 1, wsem.at[1])
    loads[2].wait()
    loads[3].wait()

    d_own[0] = rows_f[:, 0, :]
    d_own[1] = rows_f[:, 1, :]
    to_chip = remote(d_own, d_chip, 10, 10, others[1])
    to_chip.start()
    to_core = remote(d_own, d_core, 11, 11, others[0])
    to_core.start()

    def expert(mine, other, index):
        mine_at = pl.ds(pl.multiple_of(k * half, 128), half)
        other_at = pl.ds(pl.multiple_of((1 - k) * half, 128), half)
        pre = mm(mine[0], win_v[mine_at, :]) + mm(other[0], win_v[other_at, :])
        ga = mm(mine[1], wout_v[:, mine_at], NT) + mm(other[1], wout_v[:, other_at], NT)
        act, slope = gelu_parts(pre)
        act = act.astype(bf16)
        gp = (ga * slope).astype(bf16)
        po_send[index, 0] = mm(act, wout_v[:, other_at]).astype(bf16)
        po_send[index, 1] = mm(gp, win_v[other_at, :], NT).astype(bf16)
        give = remote(po_send.at[index], po_recv.at[index], 13 + index, 13 + index, others[0])
        give.start()
        acc[index, 0] = mm(act, wout_v[:, mine_at])
        acc[index, 1] = mm(gp, win_v[mine_at, :], NT)
        return give

    to_core.wait_recv()
    give0 = expert(d_own, d_core, 0)
    to_chip.wait_recv()
    forward = remote(d_chip, d_diag, 12, 12, others[0])
    forward.start()
    forward.wait_recv()
    give1 = expert(d_chip, d_diag, 1)
    give1.wait_recv()
    xs_send[...] = (acc[1] + po_recv[1].astype(f32)).astype(bf16)
    cross = remote(xs_send, xs_recv, 15, 15, others[1])
    cross.start()
    give0.wait_recv()
    total = acc[0] + po_recv[0].astype(f32)
    cross.wait_recv()
    total = (total + xs_recv[...].astype(f32)).astype(bf16)
    send_b[...] = jnp.stack([total[0], total[1]], axis=1)

    own_b = spread(send_b, rows_b, 1)
    own_b.wait()
    wait_all(rows_b, n - 1, wsem.at[3])

    slot_out = rows_b[:, 0, :]
    slot_grad = rows_b[:, 1, :]
    tok2 = tok_d[...].reshape(4 * tk, half)
    go2 = go_d[...].reshape(4 * tk, half)
    disp = disp_v[...]
    comb = comb_v[...]
    gc = comb * mm(go2, slot_out, NT)
    gd = disp * mm(tok2, slot_grad, NT)
    gl = gc - comb * jnp.sum(gc, axis=1, keepdims=True)
    gl = gl + gd - disp * jnp.sum(gd, axis=0, keepdims=True)
    gl_send[...] = gl
    gl_x = remote(gl_send, gl_recv, 16, 16, others[0])
    gl_x.start()
    first = mm(disp.astype(bf16), slot_grad)
    tok_x.wait_recv()
    gl_x.wait_recv()
    gl = (gl_send[...] + gl_recv[...]).astype(bf16)

    ef[k] = mm(gl, tok2, TN)
    ef[1 - k] = mm(gl, tok_o[...].reshape(4 * tk, half), TN)
    hn = n // 2
    mine = pl.ds(pl.multiple_of(k * hn, hn), hn)
    send_e[...] = jnp.stack([ef[0, mine, :].astype(bf16), ef[1, mine, :].astype(bf16)], axis=1)
    keeper = k == g // hn
    own_e = pltpu.make_async_copy(send_e.at[lax.rem(g, hn)], recv_e.at[g], lsem.at[8])

    def send_piece(s):
        e = lax.rem(g + lax.rem(s * stride, hn), hn)
        t = k * hn + e
        odd = lax.rem(s, 2)
        pltpu.make_async_remote_copy(
            src_ref=send_e.at[e], dst_ref=recv_e.at[g], send_sem=wsem.at[4],
            recv_sem=wsem.at[5], device_id=(t, 2 * (j + odd - 2 * j * odd) + k),
            device_id_type=MESH,
        ).start()

    def piece(s, carry):
        send_piece(s)
        return carry

    lax.fori_loop(1, hn, piece, 0)

    @pl.when(keeper)
    def _():
        own_e.start()

    @pl.when(jnp.logical_not(keeper))
    def _():
        send_piece(0)

    second = mm(gl, emb_v[:, cols(k)])
    gt_send[...] = (first + second).astype(bf16).reshape(4, tk, half)
    own_t = pltpu.make_async_copy(gt_send.at[h], gt_out.at[j, :, cols(k)], lsem.at[9])
    own_t.start()
    gt_c = []
    for i in (1, 2, 0):
        where = others[i]
        copy = remote(
            gt_send.at[2 * where[0] + where[1]], gt_out.at[j, :, cols(k)], 17 + i, 17 + i, where
        )
        copy.start()
        gt_c.append(copy)

    fin_c = [remote(fin.at[j], fin.at[j], 20 + i, 23 + j, others[i]) for i in range(3)]

    @pl.when(keeper)
    def _():
        own_e.wait()
        wait_all(recv_e, n - 1, wsem.at[5])
        rows = recv_e[...].reshape(2 * n, half)
        shape = (8, 2 * n)
        pick = lax.rem(lax.broadcasted_iota(jnp.int32, shape, 1), 2)
        pick = (pick == lax.broadcasted_iota(jnp.int32, shape, 0)).astype(bf16)
        fin[j] = mm(pick, rows)[0:2, :]
        for copy in fin_c:
            copy.start()
        for copy in fin_c:
            copy.wait_send()
        wait_all(send_e, hn - 1, wsem.at[4])
        pltpu.make_async_copy(fin.at[1 - j], fin.at[1 - j], rsem.at[24 - j]).wait()

    @pl.when(jnp.logical_not(keeper))
    def _():
        wait_all(send_e, hn, wsem.at[4])
        for chip in range(2):
            pltpu.make_async_copy(fin.at[chip], fin.at[chip], rsem.at[23 + chip]).wait()

    both = fin[0] + fin[1]
    row = jnp.where(j == 0, both[0:1, :], both[1:2, :])
    quarter = half // 2
    ge_out[...] = jnp.where(k == 0, row[:, :quarter], row[:, quarter:])

    own_t.wait()
    for copy in gt_c:
        copy.wait_recv()
    for copy in lg_c + tok_c + go_c + gt_c + [
        tok_x, to_chip, to_core, give0, give1, forward, cross, gl_x
    ]:
        copy.wait_send()
    wait_all(send_f, n - 1, wsem.at[0])
    wait_all(send_b, n - 1, wsem.at[2])


def shards(n, tokens, slot_embed, w_in, w_out, grad_out):
    images, tk, width = tokens.shape
    ff = w_in.shape[2]
    half = width // 2
    hbm = pl.BlockSpec(memory_space=pltpu.HBM)
    vm = pltpu.VMEM
    scratch = [
        vm((images, tk, width), bf16), vm((n, width), bf16), vm((width, ff), bf16),
        vm((ff, width), bf16), vm((images, tk, n), f32), vm((4, tk, n), f32),
        vm((4, tk, half), bf16), vm((4, tk, half), bf16), vm((4, tk, half), bf16),
        vm((4 * tk, n), f32), vm((4 * tk, n), f32),
        vm((n, 2, half), bf16), vm((n, 2, half), bf16),
        vm((2, n, half), bf16), vm((2, n, half), bf16), vm((2, n, half), bf16),
        vm((2, n, half), bf16),
        vm((2, 2, n, half), bf16), vm((2, 2, n, half), bf16), vm((2, 2, n, half), f32),
        vm((2, n, half), bf16), vm((2, n, half), bf16),
        vm((n, 2, half), bf16), vm((n, 2, half), bf16),
        vm((4 * tk, n), f32), vm((4 * tk, n), f32), vm((4, tk, half), bf16),
        vm((2, n, half), f32), vm((n // 2, 2, half), bf16), vm((n, 2, half), bf16),
        vm((2, 2, half), f32),
        pltpu.SemaphoreType.DMA((10,)), pltpu.SemaphoreType.DMA((25,)),
        pltpu.SemaphoreType.DMA((25,)), pltpu.SemaphoreType.DMA((6,)),
        pltpu.SemaphoreType.REGULAR((2,)),
    ]
    stride = 37 if n == 128 else 1
    nz = 8 if n == 128 else 2
    return pl.pallas_call(
        functools.partial(kernel, n, nz, stride),
        out_shape=(
            jax.ShapeDtypeStruct(tokens.shape, bf16),
            jax.ShapeDtypeStruct((1, width // 4), f32),
        ),
        in_specs=[hbm] * 5,
        out_specs=(hbm, pl.BlockSpec(memory_space=pltpu.VMEM)),
        scratch_shapes=scratch,
        compiler_params=pltpu.CompilerParams(
            collective_id=0, has_side_effects=True, vmem_limit_bytes=60 * 2**20
        ),
        cost_estimate=pl.CostEstimate(
            flops=2 * 10**9, bytes_accessed=6 * 10**6, transcendentals=10**6
        ),
    )(tokens, slot_embed, w_in, w_out, grad_out)


def solution(mesh):
    return jax.shard_map(
        functools.partial(shards, mesh.shape["expert"]),
        mesh=mesh,
        in_specs=(
            P("expert", "hidden", None),
            P(),
            P("expert", None, "hidden"),
            P("expert", "hidden", None),
            P("expert", "hidden", None),
        ),
        out_specs=(P("expert", "hidden", None), P("expert", "hidden")),
        check_vma=False,
    )
```

```python
import functools

import jax
import jax.numpy as jnp
from jax import lax
from jax.experimental import pallas as pl
from jax.experimental.pallas import tpu as pltpu
from jax.sharding import PartitionSpec as P

half_root = 0.7071067811865476
density_scale = 0.3989422804014327
MESH = pl.DeviceIdType.MESH
f32 = jnp.float32
bf16 = jnp.bfloat16
NT = (((1,), (1,)), ((), ()))
TN = (((0,), (0,)), ((), ()))
NN = (((1,), (0,)), ((), ()))


def mm(a, b, dims=NN):
    return lax.dot_general(a, b, dims, preferred_element_type=f32)


def gelu_parts(pre):
    cdf = 0.5 * (1.0 + lax.erf(pre * half_root))
    return pre * cdf, cdf + pre * jnp.exp(-0.5 * pre * pre) * density_scale


def kernel(
    n, nz, stride, tok_hbm, emb_hbm, win_hbm, wout_hbm, go_hbm, gt_out, ge_out,
    tok_v, emb_v, win_v, wout_v, lg_own, lg, tok_d, go_d, tok_o,
    disp_v, comb_v, send_f, rows_f, mine, other, win_t, wout_t,
    po_send, po_recv, acc, xs_send, xs_recv, send_b, rows_b,
    gl_send, gl_recv, gt_send, ef, send_e, recv_e, fin, lsem, ssem, rsem, wsem, fsem, here,
):
    g = lax.axis_index("expert")
    h = lax.axis_index("hidden")
    j = h // 2
    k = h % 2
    half = tok_d.shape[2]
    tk = tok_d.shape[1]
    others = [(j, 1 - k), (1 - j, k), (1 - j, 1 - k)]

    def device(where):
        return (g, 2 * where[0] + where[1])

    def cols(core):
        return pl.ds(pl.multiple_of(core * half, 128), half)

    def remote(src, dst, s, r, where):
        return pltpu.make_async_remote_copy(
            src_ref=src, dst_ref=dst, send_sem=ssem.at[s], recv_sem=rsem.at[r],
            device_id=device(where), device_id_type=MESH,
        )

    def partner(s):
        t = lax.rem(g + lax.rem(s * stride, n), n)
        odd = lax.rem(s, 2)
        return t, 2 * (j + odd - 2 * j * odd) + k

    loads = [
        pltpu.make_async_copy(tok_hbm, tok_v, lsem.at[0]),
        pltpu.make_async_copy(emb_hbm, emb_v, lsem.at[1]),
        pltpu.make_async_copy(win_hbm.at[0], win_v, lsem.at[2]),
        pltpu.make_async_copy(wout_hbm.at[0], wout_v, lsem.at[3]),
        pltpu.make_async_copy(tok_hbm.at[j, :, cols(k)], tok_d.at[h], lsem.at[4]),
        pltpu.make_async_copy(go_hbm.at[j, :, cols(k)], go_d.at[h], lsem.at[5]),
    ]
    for load in loads:
        load.start()

    zy = n // 2
    ny = zy // nz
    a = g % 2
    z = (g // 2) % nz
    y = g // (2 * nz)
    along_z = [((y * nz + (z + i) % nz) * 2 + a, h) for i in range(1, nz)]
    along_y = [((((y + i) % ny) * nz + z) * 2 + a, h) for i in range(1, ny)]
    along_x = (g + 1 - 2 * a, 2 * (1 - j) + k)

    def tell(semaphore, peer):
        pl.semaphore_signal(semaphore, inc=1, device_id=peer, device_id_type=MESH)

    barrier = pltpu.get_barrier_semaphore()
    direct = [device(where) for where in others] + along_y + along_z + [along_x]
    for peer in direct:
        tell(barrier, peer)

    loads[0].wait()
    loads[1].wait()
    for image in range(2):
        lg_own[image] = mm(tok_v[image], emb_v[...], NT)
    lg[h] = lg_own[j]
    loads[2].wait()
    win_t[...] = win_v[...].T
    loads[3].wait()
    wout_t[...] = wout_v[...].T
    pl.semaphore_wait(barrier, len(direct))
    for peer in along_z:
        tell(here.at[0], peer)

    tok_c, lg_c, go_c = [], [], []
    for i in (1, 2, 0):
        where = others[i]
        copy = remote(lg_own.at[where[0]], lg.at[h], i, i, where)
        copy.start()
        lg_c.append(copy)
    for i in (1, 2, 0):
        where = others[i]
        copy = remote(tok_hbm.at[where[0], :, cols(where[1])], tok_d.at[h], 3 + i, 3 + i, where)
        copy.start()
        tok_c.append(copy)
    for i in (1, 2, 0):
        where = others[i]
        copy = remote(go_hbm.at[where[0], :, cols(where[1])], go_d.at[h], 6 + i, 6 + i, where)
        copy.start()
        go_c.append(copy)

    for copy in lg_c:
        copy.wait_recv()
    logits = lg[...].reshape(4 * tk, n)
    col = jnp.exp(logits - jnp.max(logits, axis=0, keepdims=True))
    disp = col / jnp.sum(col, axis=0, keepdims=True)
    row = jnp.exp(logits - jnp.max(logits, axis=1, keepdims=True))
    comb = row / jnp.sum(row, axis=1, keepdims=True)
    disp_v[...] = disp
    comb_v[...] = comb

    for copy in tok_c:
        copy.wait_recv()
    loads[4].wait()
    tok_x = remote(tok_d, tok_o, 9, 9, others[0])
    tok_x.start()
    slot_rows = mm(disp.astype(bf16), tok_d[...].reshape(4 * tk, half), TN).astype(bf16)
    for copy in go_c:
        copy.wait_recv()
    loads[5].wait()
    grad_rows = mm(comb.astype(bf16), go_d[...].reshape(4 * tk, half), TN).astype(bf16)
    send_f[...] = jnp.stack([slot_rows, grad_rows], axis=1)

    if nz > 1:
        pl.semaphore_wait(here.at[0], nz - 1)
    tell(here.at[1], along_x)
    pl.semaphore_wait(here.at[1], 1)

    def wait_all(ref, count, sem):
        part = ref.at[pl.ds(0, count)]
        pltpu.make_async_copy(part, part, sem).wait()

    chunks = mine.shape[0]
    size = n // chunks
    mine_at = cols(k)
    other_at = cols(1 - k)

    def piece(chunk):
        return pl.ds(chunk * size, size)

    own_f = pltpu.make_async_copy(send_f.at[g], rows_f.at[0], lsem.at[6])
    own_f.start()
    own_b = pltpu.make_async_copy(send_b.at[0], rows_b.at[g], lsem.at[7])

    def out_chunk(chunk):
        def step(s, carry):
            t, at = partner(s)
            pltpu.make_async_remote_copy(
                src_ref=send_f.at[t], dst_ref=rows_f.at[s], send_sem=wsem.at[0],
                recv_sem=fsem.at[chunk], device_id=(t, at), device_id_type=MESH,
            ).start()
            return carry

        lax.fori_loop(max(chunk * size, 1), (chunk + 1) * size, step, 0)

    def back_chunk(chunk):
        def step(s, carry):
            t, at = partner(n - s)
            pltpu.make_async_remote_copy(
                src_ref=send_b.at[s], dst_ref=rows_b.at[g], send_sem=wsem.at[2],
                recv_sem=wsem.at[3], device_id=(t, at), device_id_type=MESH,
            ).start()
            return carry

        lax.fori_loop(max(chunk * size, 1), (chunk + 1) * size, step, 0)

    to_chip = [
        remote(mine.at[c, :, 0], mine.at[c, :, 1], 30 + c, 30 + c, others[1]) for c in range(chunks)
    ]
    to_core = [
        remote(mine.at[c], other.at[c], 40 + c, 40 + c, others[0]) for c in range(chunks)
    ]
    give = [
        remote(po_send.at[c], po_recv.at[c], 50 + c, 50 + c, others[0]) for c in range(chunks)
    ]
    cross = [
        remote(xs_send.at[c], xs_recv.at[c], 60 + c, 60 + c, others[1]) for c in range(chunks)
    ]

    def arrive(c):
        if c == 0:
            own_f.wait()
        wait_all(rows_f, size - (c == 0), fsem.at[c])
        mine[c, 0, 0] = rows_f[piece(c), 0, :]
        mine[c, 1, 0] = rows_f[piece(c), 1, :]
        to_chip[c].start()

    def share(c):
        to_chip[c].wait_recv()
        to_core[c].start()

    def expert(c):
        to_core[c].wait_recv()
        mine0 = mine[c, 0].reshape(2 * size, half)
        mine1 = mine[c, 1].reshape(2 * size, half)
        other0 = other[c, 0].reshape(2 * size, half)
        other1 = other[c, 1].reshape(2 * size, half)
        pre = mm(mine0, win_v[mine_at, :]) + mm(other0, win_v[other_at, :])
        ga = mm(mine1, wout_t[mine_at, :]) + mm(other1, wout_t[other_at, :])
        act, slope = gelu_parts(pre)
        act = act.astype(bf16)
        gp = (ga * slope).astype(bf16)
        shape = (2, size, half)
        po_send[c, 0] = mm(act, wout_v[:, other_at]).astype(bf16).reshape(shape)
        po_send[c, 1] = mm(gp, win_t[:, other_at]).astype(bf16).reshape(shape)
        give[c].start()
        acc[c, 0] = mm(act, wout_v[:, mine_at]).reshape(shape)
        acc[c, 1] = mm(gp, win_t[:, mine_at]).reshape(shape)

    def reduce(c):
        give[c].wait_recv()
        xs_send[c] = (acc[c, :, 1] + po_recv[c, :, 1].astype(f32)).astype(bf16)
        cross[c].start()

    def finish(c):
        total = acc[c, :, 0] + po_recv[c, :, 0].astype(f32)
        cross[c].wait_recv()
        total = (total + xs_recv[c].astype(f32)).astype(bf16)
        send_b[piece(c)] = jnp.stack([total[0], total[1]], axis=1)
        if c == 0:
            own_b.start()
        back_chunk(c)

    out_chunk(0)
    for slot in range(chunks + 3):
        if slot + 1 < chunks:
            out_chunk(slot + 1)
        for lag, stage in ((0, arrive), (1, share), (2, reduce), (3, finish), (1, expert)):
            if 0 <= slot - lag < chunks:
                stage(slot - lag)

    own_b.wait()
    wait_all(rows_b, n - 1, wsem.at[3])

    slot_out = rows_b[:, 0, :]
    slot_grad = rows_b[:, 1, :]
    tok2 = tok_d[...].reshape(4 * tk, half)
    go2 = go_d[...].reshape(4 * tk, half)
    disp = disp_v[...]
    comb = comb_v[...]
    gc = comb * mm(go2, slot_out, NT)
    gd = disp * mm(tok2, slot_grad, NT)
    gl = gc - comb * jnp.sum(gc, axis=1, keepdims=True)
    gl = gl + gd - disp * jnp.sum(gd, axis=0, keepdims=True)
    gl_send[...] = gl
    gl_x = remote(gl_send, gl_recv, 16, 16, others[0])
    gl_x.start()
    first = mm(disp.astype(bf16), slot_grad)
    tok_x.wait_recv()
    gl_x.wait_recv()
    gl = (gl_send[...] + gl_recv[...]).astype(bf16)

    ef[k] = mm(gl, tok2, TN)
    ef[1 - k] = mm(gl, tok_o[...].reshape(4 * tk, half), TN)
    hn = n // 2
    part = pl.ds(pl.multiple_of(k * hn, hn), hn)
    send_e[...] = jnp.stack([ef[0, part, :].astype(bf16), ef[1, part, :].astype(bf16)], axis=1)
    keeper = k == g // hn
    own_e = pltpu.make_async_copy(send_e.at[lax.rem(g, hn)], recv_e.at[g], lsem.at[8])

    def send_piece(s):
        e = lax.rem(g + lax.rem(s * stride, hn), hn)
        t = k * hn + e
        odd = lax.rem(s, 2)
        pltpu.make_async_remote_copy(
            src_ref=send_e.at[e], dst_ref=recv_e.at[g], send_sem=wsem.at[4],
            recv_sem=wsem.at[5], device_id=(t, 2 * (j + odd - 2 * j * odd) + k),
            device_id_type=MESH,
        ).start()

    def step_e(s, carry):
        send_piece(s)
        return carry

    lax.fori_loop(1, hn, step_e, 0)

    @pl.when(keeper)
    def _():
        own_e.start()

    @pl.when(jnp.logical_not(keeper))
    def _():
        send_piece(0)

    second = mm(gl, emb_v[:, cols(k)])
    gt_send[...] = (first + second).astype(bf16).reshape(4, tk, half)
    own_t = pltpu.make_async_copy(gt_send.at[h], gt_out.at[j, :, cols(k)], lsem.at[9])
    own_t.start()
    gt_c = []
    for i in (1, 2, 0):
        where = others[i]
        copy = remote(
            gt_send.at[2 * where[0] + where[1]], gt_out.at[j, :, cols(k)], 17 + i, 17 + i, where
        )
        copy.start()
        gt_c.append(copy)

    fin_c = [remote(fin.at[j], fin.at[j], 20 + i, 23 + j, others[i]) for i in range(3)]

    @pl.when(keeper)
    def _():
        own_e.wait()
        wait_all(recv_e, n - 1, wsem.at[5])
        rows = recv_e[...].reshape(2 * n, half)
        shape = (8, 2 * n)
        pick = lax.rem(lax.broadcasted_iota(jnp.int32, shape, 1), 2)
        pick = (pick == lax.broadcasted_iota(jnp.int32, shape, 0)).astype(bf16)
        fin[j] = mm(pick, rows)[0:2, :]
        for copy in fin_c:
            copy.start()
        for copy in fin_c:
            copy.wait_send()
        wait_all(send_e, hn - 1, wsem.at[4])
        pltpu.make_async_copy(fin.at[1 - j], fin.at[1 - j], rsem.at[24 - j]).wait()

    @pl.when(jnp.logical_not(keeper))
    def _():
        wait_all(send_e, hn, wsem.at[4])
        for chip in range(2):
            pltpu.make_async_copy(fin.at[chip], fin.at[chip], rsem.at[23 + chip]).wait()

    both = fin[0] + fin[1]
    row = jnp.where(j == 0, both[0:1, :], both[1:2, :])
    quarter = half // 2
    ge_out[...] = jnp.where(k == 0, row[:, :quarter], row[:, quarter:])

    own_t.wait()
    for copy in gt_c:
        copy.wait_recv()
    for copy in lg_c + tok_c + go_c + gt_c + to_chip + to_core + give + cross + [tok_x, gl_x]:
        copy.wait_send()
    wait_all(send_f, n - 1, wsem.at[0])
    wait_all(send_b, n - 1, wsem.at[2])


def shards(n, tokens, slot_embed, w_in, w_out, grad_out):
    images, tk, width = tokens.shape
    ff = w_in.shape[2]
    half = width // 2
    chunks = 4
    size = n // chunks
    hbm = pl.BlockSpec(memory_space=pltpu.HBM)
    vm = pltpu.VMEM
    scratch = [
        vm((images, tk, width), bf16), vm((n, width), bf16), vm((width, ff), bf16),
        vm((ff, width), bf16), vm((images, tk, n), f32), vm((4, tk, n), f32),
        vm((4, tk, half), bf16), vm((4, tk, half), bf16), vm((4, tk, half), bf16),
        vm((4 * tk, n), f32), vm((4 * tk, n), f32),
        vm((n, 2, half), bf16), vm((n, 2, half), bf16),
        vm((chunks, 2, 2, size, half), bf16), vm((chunks, 2, 2, size, half), bf16),
        vm((ff, width), bf16), vm((width, ff), bf16),
        vm((chunks, 2, 2, size, half), bf16), vm((chunks, 2, 2, size, half), bf16),
        vm((chunks, 2, 2, size, half), f32),
        vm((chunks, 2, size, half), bf16), vm((chunks, 2, size, half), bf16),
        vm((n, 2, half), bf16), vm((n, 2, half), bf16),
        vm((4 * tk, n), f32), vm((4 * tk, n), f32), vm((4, tk, half), bf16),
        vm((2, n, half), f32), vm((n // 2, 2, half), bf16), vm((n, 2, half), bf16),
        vm((2, 2, half), f32),
        pltpu.SemaphoreType.DMA((10,)), pltpu.SemaphoreType.DMA((70,)),
        pltpu.SemaphoreType.DMA((70,)), pltpu.SemaphoreType.DMA((6,)),
        pltpu.SemaphoreType.DMA((chunks,)),
        pltpu.SemaphoreType.REGULAR((2,)),
    ]
    stride = 37 if n == 128 else 1
    nz = 8 if n == 128 else 2
    return pl.pallas_call(
        functools.partial(kernel, n, nz, stride),
        out_shape=(
            jax.ShapeDtypeStruct(tokens.shape, bf16),
            jax.ShapeDtypeStruct((1, width // 4), f32),
        ),
        in_specs=[hbm] * 5,
        out_specs=(hbm, pl.BlockSpec(memory_space=pltpu.VMEM)),
        scratch_shapes=scratch,
        compiler_params=pltpu.CompilerParams(
            collective_id=0, has_side_effects=True, vmem_limit_bytes=60 * 2**20
        ),
        cost_estimate=pl.CostEstimate(
            flops=2 * 10**9, bytes_accessed=6 * 10**6, transcendentals=10**6
        ),
    )(tokens, slot_embed, w_in, w_out, grad_out)


def solution(mesh):
    return jax.shard_map(
        functools.partial(shards, mesh.shape["expert"]),
        mesh=mesh,
        in_specs=(
            P("expert", "hidden", None),
            P(),
            P("expert", None, "hidden"),
            P("expert", "hidden", None),
            P("expert", "hidden", None),
        ),
        out_specs=(P("expert", "hidden", None), P("expert", "hidden")),
        check_vma=False,
    )
```

```python
import functools

import jax
import jax.numpy as jnp
from jax import lax
from jax.experimental import pallas as pl
from jax.experimental.pallas import tpu as pltpu
from jax.sharding import PartitionSpec as P

half_root = 0.7071067811865476
density_scale = 0.3989422804014327
MESH = pl.DeviceIdType.MESH
f32 = jnp.float32
bf16 = jnp.bfloat16
NT = (((1,), (1,)), ((), ()))
TN = (((0,), (0,)), ((), ()))
NN = (((1,), (0,)), ((), ()))


def mm(a, b, dims=NN):
    return lax.dot_general(a, b, dims, preferred_element_type=f32)


def gelu_parts(pre):
    cdf = 0.5 * (1.0 + lax.erf(pre * half_root))
    return pre * cdf, cdf + pre * jnp.exp(-0.5 * pre * pre) * density_scale


def kernel(
    n, nz, stride, tok_hbm, emb_hbm, win_hbm, wout_hbm, go_hbm, gt_out, ge_out,
    emb_v, win_v, wout_v, lg_own, lg, tok_d, go_d, tok_o,
    disp_v, comb_v, send_f, rows_f, mine, other, win_t, wout_t,
    po_send, po_recv, acc, xs_send, xs_recv, send_b, rows_b,
    gl_send, gl_recv, gt_send, ef, send_e, recv_e, fin, lsem, ssem, rsem, wsem, fsem, here,
):
    g = lax.axis_index("expert")
    h = lax.axis_index("hidden")
    j = h // 2
    k = h % 2
    half = tok_d.shape[2]
    tk = tok_d.shape[1]
    others = [(j, 1 - k), (1 - j, k), (1 - j, 1 - k)]

    def device(where):
        return (g, 2 * where[0] + where[1])

    def cols(core):
        return pl.ds(pl.multiple_of(core * half, 128), half)

    def remote(src, dst, s, r, where):
        return pltpu.make_async_remote_copy(
            src_ref=src, dst_ref=dst, send_sem=ssem.at[s], recv_sem=rsem.at[r],
            device_id=device(where), device_id_type=MESH,
        )

    def partner(s):
        t = lax.rem(g + lax.rem(s * stride, n), n)
        odd = lax.rem(s, 2)
        return t, 2 * (j + odd - 2 * j * odd) + k

    loads = [
        None,
        pltpu.make_async_copy(emb_hbm, emb_v, lsem.at[1]),
        pltpu.make_async_copy(win_hbm.at[0], win_v, lsem.at[2]),
        pltpu.make_async_copy(wout_hbm.at[0], wout_v, lsem.at[3]),
        pltpu.make_async_copy(tok_hbm.at[j, :, cols(k)], tok_d.at[h], lsem.at[4]),
        pltpu.make_async_copy(go_hbm.at[j, :, cols(k)], go_d.at[h], lsem.at[5]),
    ]
    for i in (4, 1, 5, 2, 3):
        loads[i].start()

    zy = n // 2
    ny = zy // nz
    a = g % 2
    z = (g // 2) % nz
    y = g // (2 * nz)
    along_z = [((y * nz + (z + i) % nz) * 2 + a, h) for i in range(1, nz)]
    along_y = [((((y + i) % ny) * nz + z) * 2 + a, h) for i in range(1, ny)]
    along_x = (g + 1 - 2 * a, 2 * (1 - j) + k)

    def tell(semaphore, peer):
        pl.semaphore_signal(semaphore, inc=1, device_id=peer, device_id_type=MESH)

    barrier = pltpu.get_barrier_semaphore()
    direct = [device(where) for where in others] + along_y + along_z + [along_x]
    for peer in direct:
        tell(barrier, peer)

    pl.semaphore_wait(barrier, len(direct))

    tok_c, go_c = [], []
    for i in (1, 2, 0):
        where = others[i]
        copy = remote(tok_hbm.at[where[0], :, cols(where[1])], tok_d.at[h], 3 + i, 3 + i, where)
        copy.start()
        tok_c.append(copy)
    for i in (1, 2, 0):
        where = others[i]
        copy = remote(go_hbm.at[where[0], :, cols(where[1])], go_d.at[h], 6 + i, 6 + i, where)
        copy.start()
        go_c.append(copy)
    for peer in along_z:
        tell(here.at[0], peer)
    pl.semaphore_wait(here.at[0], nz - 1)
    tell(here.at[1], along_x)
    loads[1].wait()
    loads[2].wait()
    win_t[...] = win_v[...].T
    loads[3].wait()
    wout_t[...] = wout_v[...].T

    for copy in tok_c:
        copy.wait_recv()
    loads[4].wait()
    lg_own[...] = mm(tok_d[...].reshape(4 * tk, half), emb_v[:, cols(k)], NT)
    lg_x = remote(lg_own, lg, 0, 0, others[0])
    lg_x.start()
    tok_x = remote(tok_d, tok_o, 9, 9, others[0])
    tok_x.start()
    lg_x.wait_recv()
    logits = lg_own[...] + lg[...]
    col = jnp.exp(logits - jnp.max(logits, axis=0, keepdims=True))
    disp = col / jnp.sum(col, axis=0, keepdims=True)
    row = jnp.exp(logits - jnp.max(logits, axis=1, keepdims=True))
    comb = row / jnp.sum(row, axis=1, keepdims=True)
    disp_v[...] = disp
    comb_v[...] = comb

    slot_rows = mm(disp.astype(bf16), tok_d[...].reshape(4 * tk, half), TN).astype(bf16)
    for copy in go_c:
        copy.wait_recv()
    loads[5].wait()
    grad_rows = mm(comb.astype(bf16), go_d[...].reshape(4 * tk, half), TN).astype(bf16)
    send_f[...] = jnp.stack([slot_rows, grad_rows], axis=1)
    pl.semaphore_wait(here.at[1], 1)

    def wait_all(ref, count, sem):
        part = ref.at[pl.ds(0, count)]
        pltpu.make_async_copy(part, part, sem).wait()

    chunks = mine.shape[0]
    size = n // chunks
    mine_at = cols(k)
    other_at = cols(1 - k)

    def piece(chunk):
        return pl.ds(chunk * size, size)

    own_f = pltpu.make_async_copy(send_f.at[g], rows_f.at[0], lsem.at[6])
    own_f.start()
    own_b = pltpu.make_async_copy(send_b.at[0], rows_b.at[g], lsem.at[7])

    def out_chunk(chunk):
        def step(s, carry):
            t, at = partner(s)
            pltpu.make_async_remote_copy(
                src_ref=send_f.at[t], dst_ref=rows_f.at[s], send_sem=wsem.at[0],
                recv_sem=fsem.at[chunk], device_id=(t, at), device_id_type=MESH,
            ).start()
            return carry

        lax.fori_loop(max(chunk * size, 1), (chunk + 1) * size, step, 0)

    def back_chunk(chunk):
        def step(s, carry):
            t, at = partner(n - s)
            pltpu.make_async_remote_copy(
                src_ref=send_b.at[s], dst_ref=rows_b.at[g], send_sem=wsem.at[2],
                recv_sem=wsem.at[3], device_id=(t, at), device_id_type=MESH,
            ).start()
            return carry

        lax.fori_loop(max(chunk * size, 1), (chunk + 1) * size, step, 0)

    to_chip = [
        remote(mine.at[c, :, 0], mine.at[c, :, 1], 30 + c, 30 + c, others[1]) for c in range(chunks)
    ]
    to_core = [
        remote(mine.at[c], other.at[c], 40 + c, 40 + c, others[0]) for c in range(chunks)
    ]
    give = [
        remote(po_send.at[c], po_recv.at[c], 50 + c, 50 + c, others[0]) for c in range(chunks)
    ]
    cross = [
        remote(xs_send.at[c], xs_recv.at[c], 60 + c, 60 + c, others[1]) for c in range(chunks)
    ]

    def arrive(c):
        if c == 0:
            own_f.wait()
        wait_all(rows_f, size - (c == 0), fsem.at[c])
        mine[c, 0, 0] = rows_f[piece(c), 0, :]
        mine[c, 1, 0] = rows_f[piece(c), 1, :]
        to_chip[c].start()

    def share(c):
        to_chip[c].wait_recv()
        to_core[c].start()

    def expert(c):
        to_core[c].wait_recv()
        mine0 = mine[c, 0].reshape(2 * size, half)
        mine1 = mine[c, 1].reshape(2 * size, half)
        other0 = other[c, 0].reshape(2 * size, half)
        other1 = other[c, 1].reshape(2 * size, half)
        pre = mm(mine0, win_v[mine_at, :]) + mm(other0, win_v[other_at, :])
        ga = mm(mine1, wout_t[mine_at, :]) + mm(other1, wout_t[other_at, :])
        act, slope = gelu_parts(pre)
        act = act.astype(bf16)
        gp = (ga * slope).astype(bf16)
        shape = (2, size, half)
        po_send[c, 0] = mm(act, wout_v[:, other_at]).astype(bf16).reshape(shape)
        po_send[c, 1] = mm(gp, win_t[:, other_at]).astype(bf16).reshape(shape)
        give[c].start()
        acc[c, 0] = mm(act, wout_v[:, mine_at]).reshape(shape)
        acc[c, 1] = mm(gp, win_t[:, mine_at]).reshape(shape)

    def reduce(c):
        give[c].wait_recv()
        xs_send[c] = (acc[c, :, 1] + po_recv[c, :, 1].astype(f32)).astype(bf16)
        cross[c].start()

    def finish(c):
        total = acc[c, :, 0] + po_recv[c, :, 0].astype(f32)
        cross[c].wait_recv()
        total = (total + xs_recv[c].astype(f32)).astype(bf16)
        send_b[piece(c)] = jnp.stack([total[0], total[1]], axis=1)
        if c == 0:
            own_b.start()
        back_chunk(c)

    for c in range(chunks):
        out_chunk(c)
    order = [(arrive, 0), (arrive, 1), (arrive, 2), (arrive, 3), (share, 0), (share, 1), (expert, 0), (share, 2),
             (expert, 1), (reduce, 0), (share, 3), (expert, 2), (reduce, 1), (expert, 3), (finish, 0), (reduce, 2),
             (finish, 1), (reduce, 3), (finish, 2), (finish, 3)]
    for stage, c in order:
        stage(c)

    own_b.wait()
    wait_all(rows_b, n - 1, wsem.at[3])

    slot_out = rows_b[:, 0, :]
    slot_grad = rows_b[:, 1, :]
    tok2 = tok_d[...].reshape(4 * tk, half)
    go2 = go_d[...].reshape(4 * tk, half)
    disp = disp_v[...]
    comb = comb_v[...]
    gc = comb * mm(go2, slot_out, NT)
    gd = disp * mm(tok2, slot_grad, NT)
    gl = gc - comb * jnp.sum(gc, axis=1, keepdims=True)
    gl = gl + gd - disp * jnp.sum(gd, axis=0, keepdims=True)
    gl_send[...] = gl
    gl_x = remote(gl_send, gl_recv, 16, 16, others[0])
    gl_x.start()
    first = mm(disp.astype(bf16), slot_grad)
    tok_x.wait_recv()
    gl_x.wait_recv()
    gl = (gl_send[...] + gl_recv[...]).astype(bf16)

    ef[k] = mm(gl, tok2, TN)
    ef[1 - k] = mm(gl, tok_o[...].reshape(4 * tk, half), TN)
    hn = n // 2
    part = pl.ds(pl.multiple_of(k * hn, hn), hn)
    send_e[...] = jnp.stack([ef[0, part, :].astype(bf16), ef[1, part, :].astype(bf16)], axis=1)
    keeper = k == g // hn
    own_e = pltpu.make_async_copy(send_e.at[lax.rem(g, hn)], recv_e.at[g], lsem.at[8])

    def send_piece(s):
        e = lax.rem(g + lax.rem(s * stride, hn), hn)
        t = k * hn + e
        odd = lax.rem(s, 2)
        pltpu.make_async_remote_copy(
            src_ref=send_e.at[e], dst_ref=recv_e.at[g], send_sem=wsem.at[4],
            recv_sem=wsem.at[5], device_id=(t, 2 * (j + odd - 2 * j * odd) + k),
            device_id_type=MESH,
        ).start()

    def step_e(s, carry):
        send_piece(s)
        return carry

    lax.fori_loop(1, hn, step_e, 0)

    @pl.when(keeper)
    def _():
        own_e.start()

    @pl.when(jnp.logical_not(keeper))
    def _():
        send_piece(0)

    second = mm(gl, emb_v[:, cols(k)])
    gt_send[...] = (first + second).astype(bf16).reshape(4, tk, half)
    own_t = pltpu.make_async_copy(gt_send.at[h], gt_out.at[j, :, cols(k)], lsem.at[9])
    own_t.start()
    gt_c = []
    for i in (1, 2, 0):
        where = others[i]
        copy = remote(
            gt_send.at[2 * where[0] + where[1]], gt_out.at[j, :, cols(k)], 17 + i, 17 + i, where
        )
        copy.start()
        gt_c.append(copy)

    fin_c = [remote(fin.at[j], fin.at[j], 20 + i, 23 + j, others[i]) for i in range(3)]

    @pl.when(keeper)
    def _():
        own_e.wait()
        wait_all(recv_e, n - 1, wsem.at[5])
        rows = recv_e[...].reshape(2 * n, half)
        shape = (8, 2 * n)
        pick = lax.rem(lax.broadcasted_iota(jnp.int32, shape, 1), 2)
        pick = (pick == lax.broadcasted_iota(jnp.int32, shape, 0)).astype(bf16)
        fin[j] = mm(pick, rows)[0:2, :]
        for copy in fin_c:
            copy.start()
        for copy in fin_c:
            copy.wait_send()
        wait_all(send_e, hn - 1, wsem.at[4])
        pltpu.make_async_copy(fin.at[1 - j], fin.at[1 - j], rsem.at[24 - j]).wait()

    @pl.when(jnp.logical_not(keeper))
    def _():
        wait_all(send_e, hn, wsem.at[4])
        for chip in range(2):
            pltpu.make_async_copy(fin.at[chip], fin.at[chip], rsem.at[23 + chip]).wait()

    both = fin[0] + fin[1]
    row = jnp.where(j == 0, both[0:1, :], both[1:2, :])
    quarter = half // 2
    ge_out[...] = jnp.where(k == 0, row[:, :quarter], row[:, quarter:])

    own_t.wait()
    for copy in gt_c:
        copy.wait_recv()
    for copy in tok_c + go_c + gt_c + to_chip + to_core + give + cross + [lg_x, tok_x, gl_x]:
        copy.wait_send()
    wait_all(send_f, n - 1, wsem.at[0])
    wait_all(send_b, n - 1, wsem.at[2])


def shards(n, tokens, slot_embed, w_in, w_out, grad_out):
    images, tk, width = tokens.shape
    ff = w_in.shape[2]
    half = width // 2
    chunks = 4
    size = n // chunks
    hbm = pl.BlockSpec(memory_space=pltpu.HBM)
    vm = pltpu.VMEM
    scratch = [
        vm((n, width), bf16), vm((width, ff), bf16),
        vm((ff, width), bf16), vm((4 * tk, n), f32), vm((4 * tk, n), f32),
        vm((4, tk, half), bf16), vm((4, tk, half), bf16), vm((4, tk, half), bf16),
        vm((4 * tk, n), f32), vm((4 * tk, n), f32),
        vm((n, 2, half), bf16), vm((n, 2, half), bf16),
        vm((chunks, 2, 2, size, half), bf16), vm((chunks, 2, 2, size, half), bf16),
        vm((ff, width), bf16), vm((width, ff), bf16),
        vm((chunks, 2, 2, size, half), bf16), vm((chunks, 2, 2, size, half), bf16),
        vm((chunks, 2, 2, size, half), f32),
        vm((chunks, 2, size, half), bf16), vm((chunks, 2, size, half), bf16),
        vm((n, 2, half), bf16), vm((n, 2, half), bf16),
        vm((4 * tk, n), f32), vm((4 * tk, n), f32), vm((4, tk, half), bf16),
        vm((2, n, half), f32), vm((n // 2, 2, half), bf16), vm((n, 2, half), bf16),
        vm((2, 2, half), f32),
        pltpu.SemaphoreType.DMA((10,)), pltpu.SemaphoreType.DMA((70,)),
        pltpu.SemaphoreType.DMA((70,)), pltpu.SemaphoreType.DMA((6,)),
        pltpu.SemaphoreType.DMA((chunks,)),
        pltpu.SemaphoreType.REGULAR((2,)),
    ]
    stride = 37 if n == 128 else 1
    nz = 8 if n == 128 else 2
    results = (
        jax.ShapeDtypeStruct(tokens.shape, bf16),
        jax.ShapeDtypeStruct((1, width // 4), f32),
    )
    whole = pl.BlockSpec(memory_space=pltpu.VMEM)
    return pl.pallas_call(
        functools.partial(kernel, n, nz, stride),
        out_shape=results,
        in_specs=[hbm] * 5,
        out_specs=(hbm, whole),
        scratch_shapes=scratch,
        compiler_params=pltpu.CompilerParams(
            collective_id=0, has_side_effects=True, vmem_limit_bytes=60 * 2**20
        ),
        cost_estimate=pl.CostEstimate(
            flops=2 * 10**9, bytes_accessed=6 * 10**6, transcendentals=10**6
        ),
    )(tokens, slot_embed, w_in, w_out, grad_out)
def solution(mesh):
    return jax.shard_map(
        functools.partial(shards, mesh.shape["expert"]),
        mesh=mesh,
        in_specs=(
            P("expert", "hidden", None),
            P(),
            P("expert", None, "hidden"),
            P("expert", "hidden", None),
            P("expert", "hidden", None),
        ),
        out_specs=(P("expert", "hidden", None), P("expert", "hidden")),
        check_vma=False,
    )
```

```python
import functools

import jax
import jax.numpy as jnp
from jax import lax
from jax.experimental import pallas as pl
from jax.experimental.pallas import tpu as pltpu
from jax.sharding import PartitionSpec as P

half_root = 0.7071067811865476
density_scale = 0.3989422804014327
MESH = pl.DeviceIdType.MESH
f32 = jnp.float32
bf16 = jnp.bfloat16
NT = (((1,), (1,)), ((), ()))
TN = (((0,), (0,)), ((), ()))
NN = (((1,), (0,)), ((), ()))


def mm(a, b, dims=NN):
    return lax.dot_general(a, b, dims, preferred_element_type=f32)


def gelu_parts(pre):
    cdf = 0.5 * (1.0 + lax.erf(pre * half_root))
    return pre * cdf, cdf + pre * jnp.exp(-0.5 * pre * pre) * density_scale


def kernel(
    n, nz, stride, tok_hbm, emb_hbm, win_hbm, wout_hbm, go_hbm, gt_out, ge_out,
    emb_v, win_v, wout_v, lg_own, lg, tok_d, go_d, tok_o,
    disp_v, comb_v, send_f, rows_f, mine, other, win_t, wout_t,
    po_send, po_recv, acc, xs_send, xs_recv, send_b, rows_b,
    gl_send, gl_recv, gt_send, ef, send_e, recv_e, fin, lsem, ssem, rsem, wsem, fsem, here,
):
    g = lax.axis_index("expert")
    h = lax.axis_index("hidden")
    j = h // 2
    k = h % 2
    half = tok_d.shape[2]
    tk = tok_d.shape[1]
    others = [(j, 1 - k), (1 - j, k), (1 - j, 1 - k)]

    def device(where):
        return (g, 2 * where[0] + where[1])

    def cols(core):
        return pl.ds(pl.multiple_of(core * half, 128), half)

    def remote(src, dst, s, r, where):
        return pltpu.make_async_remote_copy(
            src_ref=src, dst_ref=dst, send_sem=ssem.at[s], recv_sem=rsem.at[r],
            device_id=device(where), device_id_type=MESH,
        )

    def partner(s):
        t = lax.rem(g + lax.rem(s * stride, n), n)
        odd = lax.rem(s, 2)
        return t, 2 * (j + odd - 2 * j * odd) + k

    loads = [
        None,
        pltpu.make_async_copy(emb_hbm, emb_v, lsem.at[1]),
        pltpu.make_async_copy(win_hbm.at[0], win_v, lsem.at[2]),
        pltpu.make_async_copy(wout_hbm.at[0], wout_v, lsem.at[3]),
        pltpu.make_async_copy(tok_hbm.at[j, :, cols(k)], tok_d.at[h], lsem.at[4]),
        pltpu.make_async_copy(go_hbm.at[j, :, cols(k)], go_d.at[h], lsem.at[5]),
    ]
    for i in (4, 1, 5, 2, 3):
        loads[i].start()

    zy = n // 2
    ny = zy // nz
    a = g % 2
    z = (g // 2) % nz
    y = g // (2 * nz)
    along_z = [((y * nz + (z + i) % nz) * 2 + a, h) for i in range(1, nz)]
    along_y = [((((y + i) % ny) * nz + z) * 2 + a, h) for i in range(1, ny)]
    along_x = (g + 1 - 2 * a, 2 * (1 - j) + k)

    def tell(semaphore, peer):
        pl.semaphore_signal(semaphore, inc=1, device_id=peer, device_id_type=MESH)

    barrier = pltpu.get_barrier_semaphore()
    direct = [device(where) for where in others] + along_y + along_z + [along_x]
    for peer in direct:
        tell(barrier, peer)

    pl.semaphore_wait(barrier, len(direct))

    tok_c, go_c = [], []
    for i in (1, 2, 0):
        where = others[i]
        copy = remote(tok_hbm.at[where[0], :, cols(where[1])], tok_d.at[h], 3 + i, 3 + i, where)
        copy.start()
        tok_c.append(copy)
    for i in (1, 2, 0):
        where = others[i]
        copy = remote(go_hbm.at[where[0], :, cols(where[1])], go_d.at[h], 6 + i, 6 + i, where)
        copy.start()
        go_c.append(copy)
    for peer in along_z:
        tell(here.at[0], peer)
    pl.semaphore_wait(here.at[0], nz - 1)
    tell(here.at[1], along_x)
    loads[1].wait()
    loads[2].wait()
    win_t[...] = win_v[...].T
    loads[3].wait()
    wout_t[...] = wout_v[...].T

    for copy in tok_c:
        copy.wait_recv()
    loads[4].wait()
    lg_own[...] = mm(tok_d[...].reshape(4 * tk, half), emb_v[:, cols(k)], NT)
    lg_x = remote(lg_own, lg, 0, 0, others[0])
    lg_x.start()
    tok_x = remote(tok_d, tok_o, 9, 9, others[0])
    tok_x.start()
    lg_x.wait_recv()
    logits = lg_own[...] + lg[...]
    col = jnp.exp(logits - jnp.max(logits, axis=0, keepdims=True))
    disp = col / jnp.sum(col, axis=0, keepdims=True)
    row = jnp.exp(logits - jnp.max(logits, axis=1, keepdims=True))
    comb = row / jnp.sum(row, axis=1, keepdims=True)
    disp_v[...] = disp
    comb_v[...] = comb

    slot_rows = mm(disp.astype(bf16), tok_d[...].reshape(4 * tk, half), TN).astype(bf16)
    for copy in go_c:
        copy.wait_recv()
    loads[5].wait()
    grad_rows = mm(comb.astype(bf16), go_d[...].reshape(4 * tk, half), TN).astype(bf16)
    send_f[...] = jnp.stack([slot_rows, grad_rows], axis=1)
    pl.semaphore_wait(here.at[1], 1)
    tell(here.at[2], device(others[0]))

    def wait_all(ref, count, sem):
        part = ref.at[pl.ds(0, count)]
        pltpu.make_async_copy(part, part, sem).wait()

    chunks = mine.shape[0]
    size = n // chunks
    mine_at = cols(k)
    other_at = cols(1 - k)

    def piece(chunk):
        return pl.ds(chunk * size, size)

    own_f = pltpu.make_async_copy(send_f.at[g], rows_f.at[0], lsem.at[6])
    own_f.start()
    own_b = pltpu.make_async_copy(send_b.at[0], rows_b.at[g], lsem.at[7])

    def out_chunk(chunk):
        def step(s, carry):
            t, at = partner(s)
            pltpu.make_async_remote_copy(
                src_ref=send_f.at[t], dst_ref=rows_f.at[s], send_sem=wsem.at[0],
                recv_sem=fsem.at[chunk], device_id=(t, at), device_id_type=MESH,
            ).start()
            return carry

        lax.fori_loop(max(chunk * size, 1), (chunk + 1) * size, step, 0)

    def back_chunk(chunk):
        def step(s, carry):
            t, at = partner(n - s)
            pltpu.make_async_remote_copy(
                src_ref=send_b.at[s], dst_ref=rows_b.at[g], send_sem=wsem.at[2],
                recv_sem=wsem.at[3], device_id=(t, at), device_id_type=MESH,
            ).start()
            return carry

        lax.fori_loop(jnp.maximum(chunk * size, 1), (chunk + 1) * size, step, 0)

    def to_chip(c):
        return remote(mine.at[c, :, 0], mine.at[c, :, 1], 30 + c, 30 + c, others[1])

    def to_core(c):
        return remote(mine.at[c], other.at[c], 40 + c, 40 + c, others[0])

    def give(c):
        return remote(po_send.at[c], po_recv.at[c], 50 + c, 50 + c, others[0])

    def cross(c):
        return remote(xs_send.at[c], xs_recv.at[c], 60 + c, 60 + c, others[1])

    def arrive(c):
        if c == 0:
            own_f.wait()
        wait_all(rows_f, size - (c == 0), fsem.at[c])
        mine[c, 0, 0] = rows_f[piece(c), 0, :]
        mine[c, 1, 0] = rows_f[piece(c), 1, :]
        to_chip(c).start()

    def share(c):
        to_chip(c).wait_recv()
        to_core(c).start()

    def expert(c):
        to_core(c).wait_recv()
        mine0 = mine[c, 0].reshape(2 * size, half)
        mine1 = mine[c, 1].reshape(2 * size, half)
        other0 = other[c, 0].reshape(2 * size, half)
        other1 = other[c, 1].reshape(2 * size, half)
        pre = mm(mine0, win_v[mine_at, :]) + mm(other0, win_v[other_at, :])
        ga = mm(mine1, wout_t[mine_at, :]) + mm(other1, wout_t[other_at, :])
        act, slope = gelu_parts(pre)
        act = act.astype(bf16)
        gp = (ga * slope).astype(bf16)
        shape = (2, size, half)
        po_send[c, 0] = mm(act, wout_v[:, other_at]).astype(bf16).reshape(shape)
        po_send[c, 1] = mm(gp, win_t[:, other_at]).astype(bf16).reshape(shape)
        give(c).start()
        acc[c, 0] = mm(act, wout_v[:, mine_at]).reshape(shape)
        acc[c, 1] = mm(gp, win_t[:, mine_at]).reshape(shape)

    def reduce(c):
        give(c).wait_recv()
        xs_send[c] = (acc[c, :, 1] + po_recv[c, :, 1].astype(f32)).astype(bf16)
        cross(c).start()

    def finish(c):
        total = acc[c, :, 0] + po_recv[c, :, 0].astype(f32)
        cross(c).wait_recv()
        total = (total + xs_recv[c].astype(f32)).astype(bf16)
        send_b[piece(c)] = jnp.stack([total[0], total[1]], axis=1)
        back_chunk(c)

    for c in range(chunks):
        out_chunk(c)
    for c in range(chunks):
        arrive(c)

    def slot(i, carry):
        for stage, lag in ((share, 0), (expert, 1), (finish, 4), (reduce, 2)):
            @pl.when(jnp.logical_and(i >= lag, i < chunks + lag))
            def _(stage=stage, lag=lag):
                stage(i - lag)

        return carry

    lax.fori_loop(0, chunks + 4, slot, 0)
    own_b.start()
    own_b.wait()
    wait_all(rows_b, n - 1, wsem.at[3])

    slot_out = rows_b[:, 0, :]
    slot_grad = rows_b[:, 1, :]
    tok2 = tok_d[...].reshape(4 * tk, half)
    go2 = go_d[...].reshape(4 * tk, half)
    disp = disp_v[...]
    comb = comb_v[...]
    gc = comb * mm(go2, slot_out, NT)
    gd = disp * mm(tok2, slot_grad, NT)
    gl = gc - comb * jnp.sum(gc, axis=1, keepdims=True)
    gl = gl + gd - disp * jnp.sum(gd, axis=0, keepdims=True)
    gl_send[...] = gl
    gl_x = remote(gl_send, gl_recv, 16, 16, others[0])
    gl_x.start()
    first = mm(disp.astype(bf16), slot_grad)
    tok_x.wait_recv()
    gl_x.wait_recv()
    gl = (gl_send[...] + gl_recv[...]).astype(bf16)

    ef[k] = mm(gl, tok2, TN)
    ef[1 - k] = mm(gl, tok_o[...].reshape(4 * tk, half), TN)
    hn = n // 2
    part = pl.ds(pl.multiple_of(k * hn, hn), hn)
    send_e[...] = jnp.stack([ef[0, part, :].astype(bf16), ef[1, part, :].astype(bf16)], axis=1)
    keeper = k == g // hn
    own_e = pltpu.make_async_copy(send_e.at[lax.rem(g, hn)], recv_e.at[lax.rem(g, hn)], lsem.at[8])
    pl.semaphore_wait(here.at[2], 1)

    def send_piece(s):
        e = lax.rem(g + lax.rem(s * stride, hn), hn)
        t = k * hn + e
        odd = lax.rem(s, 2)
        pltpu.make_async_remote_copy(
            src_ref=send_e.at[e], dst_ref=recv_e.at[lax.rem(g, hn)], send_sem=wsem.at[4],
            recv_sem=wsem.at[5], device_id=(t, 2 * (j + odd - 2 * j * odd) + g // hn),
            device_id_type=MESH,
        ).start()

    def step_e(s, carry):
        send_piece(s)
        return carry

    lax.fori_loop(1, hn, step_e, 0)

    @pl.when(keeper)
    def _():
        own_e.start()

    @pl.when(jnp.logical_not(keeper))
    def _():
        send_piece(0)

    second = mm(gl, emb_v[:, cols(k)])
    gt_send[...] = (first + second).astype(bf16).reshape(4, tk, half)
    own_t = pltpu.make_async_copy(gt_send.at[h], gt_out.at[j, :, cols(k)], lsem.at[9])
    own_t.start()
    gt_c = []
    for i in (1, 2, 0):
        where = others[i]
        copy = remote(
            gt_send.at[2 * where[0] + where[1]], gt_out.at[j, :, cols(k)], 17 + i, 17 + i, where
        )
        copy.start()
        gt_c.append(copy)

    @pl.when(keeper)
    def _():
        own_e.wait()
        wait_all(recv_e, hn - 1, wsem.at[5])
        wait_all(send_e, hn - 1, wsem.at[4])

    @pl.when(jnp.logical_not(keeper))
    def _():
        wait_all(recv_e, hn, wsem.at[5])
        wait_all(send_e, hn, wsem.at[4])

    rows = recv_e[...].reshape(2 * hn, half)
    shape = (8, 2 * hn)
    pick = lax.rem(lax.broadcasted_iota(jnp.int32, shape, 1), 2)
    pick = (pick == lax.broadcasted_iota(jnp.int32, shape, 0)).astype(bf16)
    fin[h] = mm(pick, rows)[0:2, :]
    fin_c = [remote(fin.at[h], fin.at[h], 20 + i, 23 + i, others[i]) for i in range(3)]
    for copy in fin_c:
        copy.start()
    for copy in fin_c:
        copy.wait()
    both = (fin[0] + fin[1]) + (fin[2] + fin[3])
    row = jnp.where(j == 0, both[0:1, :], both[1:2, :])
    quarter = half // 2
    ge_out[...] = jnp.where(k == 0, row[:, :quarter], row[:, quarter:])

    own_t.wait()
    for copy in gt_c:
        copy.wait_recv()
    for copy in tok_c + go_c + gt_c + [lg_x, tok_x, gl_x]:
        copy.wait_send()
    for c in range(chunks):
        for copy in (to_chip(c), to_core(c), give(c), cross(c)):
            copy.wait_send()
    wait_all(send_f, n - 1, wsem.at[0])
    wait_all(send_b, n - 1, wsem.at[2])


def shards(n, tokens, slot_embed, w_in, w_out, grad_out):
    images, tk, width = tokens.shape
    ff = w_in.shape[2]
    half = width // 2
    chunks = 4
    size = n // chunks
    hbm = pl.BlockSpec(memory_space=pltpu.HBM)
    vm = pltpu.VMEM
    scratch = [
        vm((n, width), bf16), vm((width, ff), bf16),
        vm((ff, width), bf16), vm((4 * tk, n), f32), vm((4 * tk, n), f32),
        vm((4, tk, half), bf16), vm((4, tk, half), bf16), vm((4, tk, half), bf16),
        vm((4 * tk, n), f32), vm((4 * tk, n), f32),
        vm((n, 2, half), bf16), vm((n, 2, half), bf16),
        vm((chunks, 2, 2, size, half), bf16), vm((chunks, 2, 2, size, half), bf16),
        vm((ff, width), bf16), vm((width, ff), bf16),
        vm((chunks, 2, 2, size, half), bf16), vm((chunks, 2, 2, size, half), bf16),
        vm((chunks, 2, 2, size, half), f32),
        vm((chunks, 2, size, half), bf16), vm((chunks, 2, size, half), bf16),
        vm((n, 2, half), bf16), vm((n, 2, half), bf16),
        vm((4 * tk, n), f32), vm((4 * tk, n), f32), vm((4, tk, half), bf16),
        vm((2, n, half), f32), vm((n // 2, 2, half), bf16), vm((n // 2, 2, half), bf16),
        vm((4, 2, half), f32),
        pltpu.SemaphoreType.DMA((10,)), pltpu.SemaphoreType.DMA((70,)),
        pltpu.SemaphoreType.DMA((70,)), pltpu.SemaphoreType.DMA((6,)),
        pltpu.SemaphoreType.DMA((chunks,)),
        pltpu.SemaphoreType.REGULAR((3,)),
    ]
    stride = 37 if n == 128 else 1
    nz = 8 if n == 128 else 2
    results = (
        jax.ShapeDtypeStruct(tokens.shape, bf16),
        jax.ShapeDtypeStruct((1, width // 4), f32),
    )
    whole = pl.BlockSpec(memory_space=pltpu.VMEM)
    return pl.pallas_call(
        functools.partial(kernel, n, nz, stride),
        out_shape=results,
        in_specs=[hbm] * 5,
        out_specs=(hbm, whole),
        scratch_shapes=scratch,
        compiler_params=pltpu.CompilerParams(
            collective_id=0, has_side_effects=True, vmem_limit_bytes=107 * 2**19
        ),
        cost_estimate=pl.CostEstimate(
            flops=2 * 10**9, bytes_accessed=6 * 10**6, transcendentals=10**6
        ),
    )(tokens, slot_embed, w_in, w_out, grad_out)
def solution(mesh):
    return jax.shard_map(
        functools.partial(shards, mesh.shape["expert"]),
        mesh=mesh,
        in_specs=(
            P("expert", "hidden", None),
            P(),
            P("expert", None, "hidden"),
            P("expert", "hidden", None),
            P("expert", "hidden", None),
        ),
        out_specs=(P("expert", "hidden", None), P("expert", "hidden")),
        check_vma=False,
    )
```
